32 devices in a mesh: blk: 16 (over z, x, core), tgt: 2 (over y).
Axes of the slice: x: 2, y: 2, z: 4, core: 2. Of those that a mesh axis runs over, the one named last changes fastest.
Arguments:
- queries: bfloat16 [4096, 1024], P(('blk', 'tgt')), may hold values from -6 to 6
- keys: bfloat16 [1024, 1024], P('blk'), may hold values from -6 to 6
- values: bfloat16 [1024, 1024], P('blk'), may hold values from -6 to 6
- out_weight: bfloat16 [1024, 1024], P('tgt'), may hold values from -0.1875 to 0.1875
- out_grad: bfloat16 [4096, 1024], P(('blk', 'tgt')), may hold values from -6 to 6
Outputs:
- outputs: bfloat16 [4096, 1024], P(('blk', 'tgt'))
- query_grad: bfloat16 [4096, 1024], P(('blk', 'tgt'))
- key_grad: bfloat16 [1024, 1024], P('blk', 'tgt')
- value_grad: bfloat16 [1024, 1024], P('blk', 'tgt')
- weight_grad: bfloat16 [1024, 1024], P('tgt', 'blk')
The draws below stay inside these ranges and needn't reach their ends.
All inputs are finite; a program needn't handle non-finite values.
Results may differ from the reference program's by a relative error of at most 0.017.
Values may be sent and summed in bfloat16 or wider, within the bound.
A program may use at most 64 MiB of HBM per device.

```python
import jax
import jax.numpy as jnp
from jax import lax

D = 1024
HEADS = 16
HD = 64
WIN = 5
TQ_DEV = 128
SRC_DEV = 64
QGROUP = 256
TQ = 4096
SRC = 1024
N_TGT = 2


def draw_queries(key, part):
    drawn = jax.random.normal(jax.random.fold_in(key, 1), (TQ, D), jnp.float32)
    return jnp.clip(drawn, -6.0, 6.0).astype(jnp.bfloat16)


def draw_keys(key, part):
    drawn = jax.random.normal(jax.random.fold_in(key, 2), (SRC, D), jnp.float32)
    return jnp.clip(drawn, -6.0, 6.0).astype(jnp.bfloat16)


def with_spikes(drawn, rng, source, target, blocks, factor):
    def block_of(axis_at):
        return (jnp.arange(drawn.shape[axis_at]) // (drawn.shape[axis_at] // blocks)).reshape((-1,) + (1,) * (drawn.ndim - 1 - axis_at))

    first = jax.random.permutation(rng, blocks)[block_of(target)]
    far = (block_of(target) + blocks // 2) % blocks
    return jnp.where((block_of(source) == first) | (block_of(source) == far), factor * drawn, drawn)


def steps_of(rng, dims, cuts, smallest, top_value):
    factor_of, own = 1.0, jax.random.fold_in(rng, 6)
    for position, parts in cuts:
        steps = jnp.exp(jax.random.uniform(jax.random.fold_in(own, position), (parts,), jnp.float32, smallest / len(cuts), top_value / len(cuts)))
        factor_of = factor_of * jnp.repeat(steps, dims[position] // parts).reshape([-1 if axis == position else 1 for axis in range(len(dims))])
    return factor_of


def centred(rng, dims, deviation, reach, split=(), kind=jnp.bfloat16):
    array = deviation * jax.random.normal(rng, dims, jnp.float32)
    if split:
        array = array * steps_of(rng, dims, split, -0.22, 0.18)
    return jnp.clip(array, -reach, reach).astype(kind)


def gaussian_with(stream_key, extent, spread, limit, shards, heavy, kind=jnp.bfloat16):
    values = spread * jax.random.normal(stream_key, extent, jnp.float32)
    if shards:
        values = values * steps_of(stream_key, extent, shards, -0.22, 0.18)
    return jnp.clip(with_spikes(values, jax.random.fold_in(stream_key, 3), *heavy), -limit, limit).astype(kind)


def setup_inputs(seed: int = 0) -> dict:
    key_of = jax.random.split(jax.random.key(seed), 6)
    return {
        "queries": draw_queries(jax.random.fold_in(key_of[5], 71), 0),
        "keys": draw_keys(jax.random.fold_in(key_of[5], 71), 0),
        "values": centred(key_of[2], (SRC, D), 1.0, 6.0, ((0, 16),)),
        "out_weight": centred(key_of[3], (D, D), D ** -0.5, 0.1875, ((0, 2),)),
        "out_grad": gaussian_with(key_of[4], (TQ, D), 1.0, 6.0, ((0, 32),), (0, 1, 32, 2.75)),
    }


def attend_group(query_rows, key_rows, value_rows, grad_rows):
    scale = HD ** -0.5
    count = query_rows.shape[0]
    width = key_rows.shape[0]
    query_heads = query_rows.astype(jnp.float32).reshape(count, HEADS, HD)
    key_heads = key_rows.astype(jnp.float32).reshape(width, HEADS, HD)
    value_heads = value_rows.astype(jnp.float32).reshape(width, HEADS, HD)
    grad_heads = grad_rows.astype(jnp.float32).reshape(count, HEADS, HD)
    scores = jnp.einsum("rhd,jhd->hrj", query_heads, key_heads) * scale
    top = jnp.max(scores, axis=-1, keepdims=True)
    expo = jnp.exp(scores - top)
    probs = expo / jnp.sum(expo, axis=-1, keepdims=True)
    probs_low = probs.astype(jnp.bfloat16).astype(jnp.float32)
    attended = jnp.einsum("hrj,jhd->rhd", probs_low, value_heads).reshape(count, D).astype(jnp.bfloat16)
    prob_grad = jnp.einsum("rhd,jhd->hrj", grad_heads, value_heads)
    center = jnp.sum(probs * prob_grad, axis=-1, keepdims=True)
    score_grad = (scale * probs * (prob_grad - center)).astype(jnp.bfloat16).astype(jnp.float32)
    query_grad = jnp.einsum("hrj,jhd->rhd", score_grad, key_heads).reshape(count, D).astype(jnp.bfloat16)
    key_part = jnp.einsum("hrj,rhd->jhd", score_grad, query_heads).reshape(width, D)
    value_part = jnp.einsum("hrj,rhd->jhd", probs_low, grad_heads).reshape(width, D)
    return attended, query_grad, key_part, value_part


def reference(queries, keys, values, out_weight, out_grad):
    groups = SRC // SRC_DEV
    attended_grad = jnp.dot(out_grad, out_weight.T, preferred_element_type=jnp.float32).astype(jnp.bfloat16)

    def step(carry, index):
        key_grad, value_grad, weight_grad = carry
        start = (index * QGROUP).astype(jnp.int32)
        query_rows = lax.dynamic_slice_in_dim(queries, start, QGROUP, 0)
        grad_rows = lax.dynamic_slice_in_dim(attended_grad, start, QGROUP, 0)
        cot_rows = lax.dynamic_slice_in_dim(out_grad, start, QGROUP, 0)
        starts = [(((index - w) % groups) * SRC_DEV).astype(jnp.int32) for w in range(WIN)]
        key_rows = jnp.concatenate([lax.dynamic_slice_in_dim(keys, s, SRC_DEV, 0) for s in starts], axis=0)
        value_rows = jnp.concatenate([lax.dynamic_slice_in_dim(values, s, SRC_DEV, 0) for s in starts], axis=0)
        attended, query_grad, key_part, value_part = attend_group(query_rows, key_rows, value_rows, grad_rows)
        out_rows = jnp.dot(attended, out_weight, preferred_element_type=jnp.float32).astype(jnp.bfloat16)
        tiles_att = attended.astype(jnp.float32).reshape(N_TGT, TQ_DEV, D)
        tiles_cot = cot_rows.astype(jnp.float32).reshape(N_TGT, TQ_DEV, D)
        partial_value = jnp.einsum("trc,tre->tce", tiles_att, tiles_cot).astype(jnp.bfloat16).astype(jnp.float32)
        weight_grad = weight_grad + jnp.sum(partial_value, axis=0)
        for w in range(WIN):
            old_k = lax.dynamic_slice_in_dim(key_grad, starts[w], SRC_DEV, 0)
            key_grad = lax.dynamic_update_slice_in_dim(key_grad, old_k + key_part[w * SRC_DEV:(w + 1) * SRC_DEV], starts[w], 0)
            old_v = lax.dynamic_slice_in_dim(value_grad, starts[w], SRC_DEV, 0)
            value_grad = lax.dynamic_update_slice_in_dim(value_grad, old_v + value_part[w * SRC_DEV:(w + 1) * SRC_DEV], starts[w], 0)
        return (key_grad, value_grad, weight_grad), (out_rows, query_grad)

    init = (jnp.zeros((SRC, D), jnp.float32), jnp.zeros((SRC, D), jnp.float32), jnp.zeros((D, D), jnp.float32))
    (key_grad, value_grad, weight_grad), (out_all, query_all) = lax.scan(step, init, jnp.arange(groups, dtype=jnp.int32))
    outputs = out_all.reshape(TQ, D)
    query_grad = query_all.reshape(TQ, D)
    return outputs, query_grad, key_grad.astype(jnp.bfloat16), value_grad.astype(jnp.bfloat16), weight_grad.astype(jnp.bfloat16)
```

```python
import functools

import jax
import jax.numpy as jnp
from jax import lax
from jax.experimental import pallas as pl
from jax.experimental.pallas import tpu as pltpu
from jax.sharding import PartitionSpec as P

HD = 64
WIN = 5
LANES = 128
BF = jnp.bfloat16
F32 = jnp.float32
MESH = pl.DeviceIdType.MESH


def dot(a, b, ca, cb):
    return lax.dot_general(a, b, (((ca,), (cb,)), ((), ())), preferred_element_type=F32)


def kernel(
    N,
    T,
    nbits,
    q_ref,
    k_ref,
    v_ref,
    w_ref,
    og_ref,
    out_ref,
    qg_ref,
    kg_ref,
    vg_ref,
    wgt_ref,
    qall,
    ogall,
    ogt,
    kall,
    vall,
    ag,
    att,
    qgs,
    kvown,
    kvs,
    kvr,
    outs,
    outr,
    outown,
    *rest,
):
    acc = rest[:nbits]
    ws = rest[nbits : 2 * nbits]
    wr = rest[2 * nbits : 3 * nbits]
    q_ss, q_rs, og_ss, og_rs, kv_ss, kv_rs, kvg_ss, kvg_rs, qg_ss, qg_rs, o_ss, o_rs, w_ss, w_rs = rest[
        3 * nbits :
    ]
    b = lax.axis_index("blk")
    t = lax.axis_index("tgt")
    rows, D = q_ref.shape
    Dt = w_ref.shape[0]
    R = rows * T
    src = k_ref.shape[0]
    pairs = Dt // LANES
    EB = D // N
    scale = HD ** (-0.5)

    def blk_at(step):
        return lax.rem(b + step + N, N)

    def tgt_at(step):
        return lax.rem(t + step + T, T)

    def bit(k):
        return lax.rem(b // (1 << k), 2)

    def mirror(k):
        return b + (1 - 2 * bit(k)) * (1 << k)

    def cols(tt):
        return pl.ds(pl.multiple_of(tt * Dt, LANES), Dt)

    def tile(tt):
        return pl.ds(pl.multiple_of(tt * rows, LANES), rows)

    def lanes(p, base=0):
        return pl.ds(pl.multiple_of(base + p * LANES, LANES), LANES)

    def remote(src_, dst_, ss, rs, dev):
        return pltpu.make_async_remote_copy(
            src_ref=src_, dst_ref=dst_, send_sem=ss, recv_sem=rs, device_id=dev, device_id_type=MESH
        )

    def q_copy(d):
        other = tgt_at(d)
        return remote(q_ref.at[:, cols(other)], qall.at[tile(t), :], q_ss.at[d], q_rs.at[d], (b, other))

    def og_copy(d):
        return remote(og_ref, ogall.at[tile(t), :], og_ss.at[d], og_rs.at[d], (b, tgt_at(d)))

    def kv_copy(i, w):
        ref, dst = ((k_ref, kall), (v_ref, vall))[i]
        return remote(
            ref.at[:, cols(t)],
            dst.at[pl.ds(w * src, src), :],
            kv_ss.at[i, w],
            kv_rs.at[i, w],
            (blk_at(w), t),
        )

    def kvg_copy(p, w):
        return remote(
            kvs.at[w - 1, :, :, lanes(p)],
            kvr.at[w - 1, :, :, lanes(p)],
            kvg_ss.at[p, w],
            kvg_rs.at[p, w],
            (blk_at(-w), t),
        )

    def qg_copy(p, d):
        other = tgt_at(d)
        return remote(
            qgs.at[tile(other), lanes(p)],
            qg_ref.at[:, lanes(p, t * Dt)],
            qg_ss.at[p, d],
            qg_rs.at[p, d],
            (b, other),
        )

    def o_copy(d):
        return remote(outs.at[d - 1], outr.at[d - 1], o_ss.at[d], o_rs.at[d], (b, tgt_at(d)))

    def w_copy(k, p):
        return remote(ws[k].at[p], wr[k].at[p], w_ss.at[k, p], w_rs.at[k, p], (mirror(k), t))

    barrier = pltpu.get_barrier_semaphore()
    peers = [(b, tgt_at(d)) for d in range(1, T)]
    for w in range(1, WIN):
        peers += [(blk_at(w), t), (blk_at(-w), t)]
    for k in range(3, nbits):
        peers.append((mirror(k), t))
    for peer in peers:
        pl.semaphore_signal(barrier, inc=1, device_id=peer, device_id_type=MESH)
    pl.semaphore_wait(barrier, len(peers))

    for d in range(1, T):
        og_copy(d).start()
    for w in range(WIN - 1, 0, -1):
        kv_copy(0, w).start()
        kv_copy(1, w).start()
    for d in range(1, T):
        q_copy(d).start()

    def project(tt):
        part = ogall[tile(tt), :]
        ag[tile(tt), :] = dot(part, w_ref[...], 1, 1).astype(BF)
        ogt[:, tile(tt)] = part.astype(F32).T.astype(BF)

    ogall[tile(t), :] = og_ref[...]
    qall[tile(t), :] = q_ref[:, cols(t)]
    kall[pl.ds(0, src), :] = k_ref[:, cols(t)]
    vall[pl.ds(0, src), :] = v_ref[:, cols(t)]
    project(t)
    for d in range(1, T):
        og_copy(d).wait_recv()
        project(tgt_at(-d))
    for d in range(1, T):
        q_copy(d).wait_recv()
    for w in range(WIN - 1, 0, -1):
        kv_copy(0, w).wait_recv()
        kv_copy(1, w).wait_recv()

    half = lax.broadcasted_iota(jnp.int32, (1, LANES), 1) // HD

    def fold(k, p):
        w_copy(k, p).wait_recv()
        value = acc[k][p, :, bit(k)] + wr[k][p].astype(F32)
        if k + 1 < nbits:
            acc[k + 1][p] = value.reshape(N >> (k + 2), 2, EB, LANES)
            ws[k + 1][p] = acc[k + 1][p, :, 1 - bit(k + 1)].astype(BF)
            w_copy(k + 1, p).start()
        else:
            wgt_ref[:, lanes(p)] = value[0].astype(BF)

    def pair(p, carry):
        c = lanes(p)
        kp, vp, qp, gp = kall[:, c], vall[:, c], qall[:, c], ag[:, c]
        att_t = jnp.zeros((LANES, R), F32)
        qg_t = jnp.zeros((LANES, R), F32)
        kg = jnp.zeros((WIN * src, LANES), F32)
        vg = jnp.zeros((WIN * src, LANES), F32)
        for i in range(2):
            mask = (half == i).astype(F32).astype(BF)
            km, vm, qm, gm = kp * mask, vp * mask, qp * mask, gp * mask
            scores = dot(km, qp, 1, 1) * scale
            expo = jnp.exp(scores - jnp.max(scores, axis=0, keepdims=True))
            probs = expo * (1.0 / jnp.sum(expo, axis=0, keepdims=True))
            low = probs.astype(BF)
            prob_grad = dot(vm, gp, 1, 1)
            center = jnp.sum(probs * prob_grad, axis=0, keepdims=True)
            score_grad = (scale * probs * (prob_grad - center)).astype(BF)
            att_t += dot(vm, low, 0, 0)
            qg_t += dot(km, score_grad, 0, 0)
            kg += dot(score_grad, qm, 1, 0)
            vg += dot(low, gm, 1, 0)
        att_low = att_t.astype(BF)
        grad = dot(ogt[...], att_low, 1, 1)
        acc[0][p] = grad.reshape(N // 2, 2, EB, LANES)
        ws[0][p] = acc[0][p, :, 1 - bit(0)].astype(BF)
        w_copy(0, p).start()
        kvown[0, :, c] = kg[:src]
        kvown[1, :, c] = vg[:src]
        for w in range(1, WIN):
            kvs[w - 1, 0, :, c] = kg[w * src : (w + 1) * src].astype(BF)
            kvs[w - 1, 1, :, c] = vg[w * src : (w + 1) * src].astype(BF)
            kvg_copy(p, w).start()
        qgs[:, c] = qg_t.T.astype(BF)
        for d in range(1, T):
            qg_copy(p, d).start()
        att[:, c] = att_t.T.astype(BF)

        @pl.when(p >= 1)
        def _():
            fold(0, p - 1)

        @pl.when(p >= 2)
        def _():
            fold(1, p - 2)

        return carry

    lax.fori_loop(0, pairs, pair, 0)

    fold(0, pairs - 1)
    for d in range(1, T):
        outs[d - 1] = dot(att[tile(tgt_at(d)), :], w_ref[...], 1, 0).astype(BF)
        o_copy(d).start()
    for p in range(max(pairs - 2, 0), pairs):
        fold(1, p)
    outown[...] = dot(att[tile(t), :], w_ref[...], 1, 0)
    qg_ref[:, cols(t)] = qgs[tile(t), :]
    for k in range(2, nbits):
        for p in range(pairs):
            fold(k, p)
        if k == 2:
            for p in range(pairs):
                for w in range(1, WIN):
                    kvg_copy(p, w).wait_recv()
            for i, ref in enumerate((kg_ref, vg_ref)):
                total = kvown[i]
                for w in range(1, WIN):
                    total += kvr[w - 1, i].astype(F32)
                ref[...] = total.astype(BF)
    total = outown[...]
    for d in range(1, T):
        o_copy(d).wait_recv()
        total += outr[d - 1].astype(F32)
    out_ref[...] = total.astype(BF)
    for p in range(pairs):
        for d in range(1, T):
            qg_copy(p, d).wait_recv()

    for d in range(1, T):
        og_copy(d).wait_send()
        q_copy(d).wait_send()
        o_copy(d).wait_send()
    for w in range(1, WIN):
        kv_copy(0, w).wait_send()
        kv_copy(1, w).wait_send()
    for p in range(pairs):
        for w in range(1, WIN):
            kvg_copy(p, w).wait_send()
        for d in range(1, T):
            qg_copy(p, d).wait_send()
        for k in range(nbits):
            w_copy(k, p).wait_send()


def local(queries, keys, values, out_weight, out_grad):
    N = lax.axis_size("blk")
    T = lax.axis_size("tgt")
    nbits = N.bit_length() - 1
    rows, D = queries.shape
    src = keys.shape[0]
    Dt = out_weight.shape[0]
    R = rows * T
    pairs = Dt // LANES
    EB = D // N
    halves = [(pairs, N >> (k + 1), EB, LANES) for k in range(nbits)]
    scratch = [
        pltpu.VMEM((R, Dt), BF),
        pltpu.VMEM((R, D), BF),
        pltpu.VMEM((D, R), BF),
        pltpu.VMEM((WIN * src, Dt), BF),
        pltpu.VMEM((WIN * src, Dt), BF),
        pltpu.VMEM((R, Dt), BF),
        pltpu.VMEM((R, Dt), BF),
        pltpu.VMEM((R, Dt), BF),
        pltpu.VMEM((2, src, Dt), F32),
        pltpu.VMEM((WIN - 1, 2, src, Dt), BF),
        pltpu.VMEM((WIN - 1, 2, src, Dt), BF),
        pltpu.VMEM((T - 1, rows, D), BF),
        pltpu.VMEM((T - 1, rows, D), BF),
        pltpu.VMEM((rows, D), F32),
    ]
    scratch += [pltpu.VMEM((h[0], h[1], 2, EB, LANES), F32) for h in halves]
    scratch += [pltpu.VMEM(h, BF) for h in halves]
    scratch += [pltpu.VMEM(h, BF) for h in halves]
    for shape in ((T,), (T,), (2, WIN), (pairs, WIN), (pairs, T), (T,), (nbits, pairs)):
        scratch += [pltpu.SemaphoreType.DMA(shape)] * 2
    vmem = pl.BlockSpec(memory_space=pltpu.VMEM)
    out, qg, kg, vg, wgt = pl.pallas_call(
        functools.partial(kernel, N, T, nbits),
        out_shape=(
            jax.ShapeDtypeStruct((rows, D), BF),
            jax.ShapeDtypeStruct((rows, D), BF),
            jax.ShapeDtypeStruct((src, Dt), BF),
            jax.ShapeDtypeStruct((src, Dt), BF),
            jax.ShapeDtypeStruct((EB, Dt), BF),
        ),
        in_specs=[vmem] * 5,
        out_specs=(vmem,) * 5,
        scratch_shapes=scratch,
        compiler_params=pltpu.CompilerParams(
            collective_id=0, has_side_effects=True, vmem_limit_bytes=48 * 1024 * 1024
        ),
    )(queries, keys, values, out_weight, out_grad)
    return out, qg, kg, vg, wgt.T


def solution(mesh):
    return jax.shard_map(
        local,
        mesh=mesh,
        in_specs=(
            P(("blk", "tgt"), None),
            P("blk", None),
            P("blk", None),
            P("tgt", None),
            P(("blk", "tgt"), None),
        ),
        out_specs=(
            P(("blk", "tgt"), None),
            P(("blk", "tgt"), None),
            P("blk", "tgt"),
            P("blk", "tgt"),
            P("tgt", "blk"),
        ),
        check_vma=False,
    )
```

```python
import functools

import jax
import jax.numpy as jnp
from jax import lax
from jax.experimental import pallas as pl
from jax.experimental.pallas import tpu as pltpu
from jax.sharding import PartitionSpec as P

HD = 64
WIN = 5
LANES = 128
BF = jnp.bfloat16
F32 = jnp.float32
MESH = pl.DeviceIdType.MESH


def dot(a, b, ca, cb):
    return lax.dot_general(a, b, (((ca,), (cb,)), ((), ())), preferred_element_type=F32)


def kernel(
    N,
    T,
    nbits,
    q_ref,
    k_ref,
    v_ref,
    w_ref,
    og_ref,
    out_ref,
    qg_ref,
    kg_ref,
    vg_ref,
    wgt_ref,
    qall,
    ogall,
    ogt,
    kall,
    vall,
    wv,
    in_s,
    ag,
    att,
    qgs,
    kvown,
    kvs,
    kvr,
    outs,
    outr,
    outown,
    *rest,
):
    acc = rest[:nbits]
    ws = rest[nbits : 2 * nbits]
    wr = rest[2 * nbits : 3 * nbits]
    q_ss, q_rs, og_ss, og_rs, kv_ss, kv_rs, kvg_ss, kvg_rs, qg_ss, qg_rs, o_ss, o_rs, w_ss, w_rs = rest[
        3 * nbits :
    ]
    b = lax.axis_index("blk")
    t = lax.axis_index("tgt")
    rows, D = q_ref.shape
    Dt = w_ref.shape[0]
    R = rows * T
    src = k_ref.shape[0]
    pairs = Dt // LANES
    EB = D // N
    scale = HD ** (-0.5)

    def blk_at(step):
        return lax.rem(b + step + N, N)

    def tgt_at(step):
        return lax.rem(t + step + T, T)

    def bit(k):
        return lax.rem(b // (1 << k), 2)

    def mirror(k):
        return b + (1 - 2 * bit(k)) * (1 << k)

    def cols(tt):
        return pl.ds(pl.multiple_of(tt * Dt, LANES), Dt)

    def tile(tt):
        return pl.ds(pl.multiple_of(tt * rows, LANES), rows)

    def lanes(p, base=0):
        return pl.ds(pl.multiple_of(base + p * LANES, LANES), LANES)

    def remote(src_, dst_, ss, rs, dev):
        return pltpu.make_async_remote_copy(
            src_ref=src_, dst_ref=dst_, send_sem=ss, recv_sem=rs, device_id=dev, device_id_type=MESH
        )

    def q_copy(d):
        other = tgt_at(d)
        return remote(q_ref.at[:, cols(other)], qall.at[tile(t), :], q_ss.at[d], q_rs.at[d], (b, other))

    def og_copy(d):
        return remote(og_ref, ogall.at[tile(t), :], og_ss.at[d], og_rs.at[d], (b, tgt_at(d)))

    def kv_copy(i, w):
        ref, dst = ((k_ref, kall), (v_ref, vall))[i]
        return remote(
            ref.at[:, cols(t)],
            dst.at[pl.ds(w * src, src), :],
            kv_ss.at[i, w],
            kv_rs.at[i, w],
            (blk_at(w), t),
        )

    def kvg_copy(p, w):
        return remote(
            kvs.at[w - 1, :, :, lanes(p)],
            kvr.at[w - 1, :, :, lanes(p)],
            kvg_ss.at[p, w],
            kvg_rs.at[p, w],
            (blk_at(-w), t),
        )

    def qg_copy(p, d):
        other = tgt_at(d)
        return remote(
            qgs.at[tile(other), lanes(p)],
            qg_ref.at[:, lanes(p, t * Dt)],
            qg_ss.at[p, d],
            qg_rs.at[p, d],
            (b, other),
        )

    def o_copy(d):
        return remote(outs.at[d - 1], outr.at[d - 1], o_ss.at[d], o_rs.at[d], (b, tgt_at(d)))

    def w_copy(k, p):
        return remote(ws[k].at[p], wr[k].at[p], w_ss.at[k, p], w_rs.at[k, p], (mirror(k), t))

    own = [
        pltpu.make_async_copy(s, d, in_s.at[i])
        for i, (s, d) in enumerate(
            (
                (og_ref, ogall.at[tile(t), :]),
                (w_ref, wv),
                (q_ref.at[:, cols(t)], qall.at[tile(t), :]),
                (k_ref.at[:, cols(t)], kall.at[pl.ds(0, src), :]),
                (v_ref.at[:, cols(t)], vall.at[pl.ds(0, src), :]),
            )
        )
    ]
    for copy in own:
        copy.start()

    barrier = pltpu.get_barrier_semaphore()
    peers = [(b, tgt_at(d)) for d in range(1, T)]
    for w in range(1, WIN):
        peers += [(blk_at(w), t), (blk_at(-w), t)]
    for k in range(3, nbits):
        peers.append((mirror(k), t))
    for peer in peers:
        pl.semaphore_signal(barrier, inc=1, device_id=peer, device_id_type=MESH)
    pl.semaphore_wait(barrier, len(peers))

    for d in range(1, T):
        og_copy(d).start()
    for w in range(WIN - 1, 0, -1):
        kv_copy(0, w).start()
        kv_copy(1, w).start()
    for d in range(1, T):
        q_copy(d).start()

    def project(tt):
        part = ogall[tile(tt), :]
        ag[tile(tt), :] = dot(part, wv[...], 1, 1).astype(BF)
        ogt[:, tile(tt)] = part.astype(F32).T.astype(BF)

    for copy in own:
        copy.wait()
    project(t)
    for d in range(1, T):
        og_copy(d).wait_recv()
        project(tgt_at(-d))
    for d in range(1, T):
        q_copy(d).wait_recv()
    for w in range(WIN - 1, 0, -1):
        kv_copy(0, w).wait_recv()
        kv_copy(1, w).wait_recv()

    half = lax.broadcasted_iota(jnp.int32, (1, LANES), 1) // HD

    def fold(k, p):
        w_copy(k, p).wait_recv()
        value = acc[k][p, :, bit(k)] + wr[k][p].astype(F32)
        if k + 1 < nbits:
            acc[k + 1][p] = value.reshape(N >> (k + 2), 2, EB, LANES)
            ws[k + 1][p] = acc[k + 1][p, :, 1 - bit(k + 1)].astype(BF)
            w_copy(k + 1, p).start()
        else:
            wgt_ref[:, lanes(p)] = value[0].astype(BF)

    def pair(p, carry):
        c = lanes(p)
        kp, vp, qp, gp = kall[:, c], vall[:, c], qall[:, c], ag[:, c]
        att_t = jnp.zeros((LANES, R), F32)
        qg_t = jnp.zeros((LANES, R), F32)
        kg = jnp.zeros((WIN * src, LANES), F32)
        vg = jnp.zeros((WIN * src, LANES), F32)
        for i in range(2):
            mask = (half == i).astype(F32).astype(BF)
            km, vm, qm, gm = kp * mask, vp * mask, qp * mask, gp * mask
            scores = dot(km, qp, 1, 1) * scale
            expo = jnp.exp(scores - jnp.max(scores, axis=0, keepdims=True))
            probs = expo * (1.0 / jnp.sum(expo, axis=0, keepdims=True))
            low = probs.astype(BF)
            prob_grad = dot(vm, gp, 1, 1)
            center = jnp.sum(probs * prob_grad, axis=0, keepdims=True)
            score_grad = (scale * probs * (prob_grad - center)).astype(BF)
            att_t += dot(vm, low, 0, 0)
            qg_t += dot(km, score_grad, 0, 0)
            kg += dot(score_grad, qm, 1, 0)
            vg += dot(low, gm, 1, 0)
        att_low = att_t.astype(BF)
        grad = dot(ogt[...], att_low, 1, 1)
        acc[0][p] = grad.reshape(N // 2, 2, EB, LANES)
        ws[0][p] = acc[0][p, :, 1 - bit(0)].astype(BF)
        w_copy(0, p).start()
        kvown[0, :, c] = kg[:src]
        kvown[1, :, c] = vg[:src]
        for w in range(1, WIN):
            kvs[w - 1, 0, :, c] = kg[w * src : (w + 1) * src].astype(BF)
            kvs[w - 1, 1, :, c] = vg[w * src : (w + 1) * src].astype(BF)
            kvg_copy(p, w).start()
        qgs[:, c] = qg_t.T.astype(BF)
        for d in range(1, T):
            qg_copy(p, d).start()
        att[:, c] = att_t.T.astype(BF)

        @pl.when(p >= 1)
        def _():
            fold(0, p - 1)

        @pl.when(p >= 2)
        def _():
            fold(1, p - 2)

        return carry

    lax.fori_loop(0, pairs, pair, 0)

    fold(0, pairs - 1)
    for d in range(1, T):
        outs[d - 1] = dot(att[tile(tgt_at(d)), :], wv[...], 1, 0).astype(BF)
        o_copy(d).start()
    for p in range(max(pairs - 2, 0), pairs):
        fold(1, p)
    outown[...] = dot(att[tile(t), :], wv[...], 1, 0)
    qg_ref[:, cols(t)] = qgs[tile(t), :]
    for k in range(2, nbits):
        for p in range(pairs):
            fold(k, p)
        if k == 2:
            for p in range(pairs):
                for w in range(1, WIN):
                    kvg_copy(p, w).wait_recv()
            for i, ref in enumerate((kg_ref, vg_ref)):
                total = kvown[i]
                for w in range(1, WIN):
                    total += kvr[w - 1, i].astype(F32)
                ref[...] = total.astype(BF)
    total = outown[...]
    for d in range(1, T):
        o_copy(d).wait_recv()
        total += outr[d - 1].astype(F32)
    out_ref[...] = total.astype(BF)
    for p in range(pairs):
        for d in range(1, T):
            qg_copy(p, d).wait_recv()

    for d in range(1, T):
        og_copy(d).wait_send()
        q_copy(d).wait_send()
        o_copy(d).wait_send()
    for w in range(1, WIN):
        kv_copy(0, w).wait_send()
        kv_copy(1, w).wait_send()
    for p in range(pairs):
        for w in range(1, WIN):
            kvg_copy(p, w).wait_send()
        for d in range(1, T):
            qg_copy(p, d).wait_send()
        for k in range(nbits):
            w_copy(k, p).wait_send()


def store_kernel(*refs):
    copies = [pltpu.make_async_copy(refs[i], refs[5 + i], refs[10].at[i]) for i in range(5)]
    for copy in copies:
        copy.start()
    for copy in copies:
        copy.wait()


def local(queries, keys, values, out_weight, out_grad):
    N = lax.axis_size("blk")
    T = lax.axis_size("tgt")
    nbits = N.bit_length() - 1
    rows, D = queries.shape
    src = keys.shape[0]
    Dt = out_weight.shape[0]
    R = rows * T
    pairs = Dt // LANES
    EB = D // N
    halves = [(pairs, N >> (k + 1), EB, LANES) for k in range(nbits)]
    scratch = [
        pltpu.VMEM((R, Dt), BF),
        pltpu.VMEM((R, D), BF),
        pltpu.VMEM((D, R), BF),
        pltpu.VMEM((WIN * src, Dt), BF),
        pltpu.VMEM((WIN * src, Dt), BF),
        pltpu.VMEM((Dt, D), BF),
        pltpu.SemaphoreType.DMA((5,)),
        pltpu.VMEM((R, Dt), BF),
        pltpu.VMEM((R, Dt), BF),
        pltpu.VMEM((R, Dt), BF),
        pltpu.VMEM((2, src, Dt), F32),
        pltpu.VMEM((WIN - 1, 2, src, Dt), BF),
        pltpu.VMEM((WIN - 1, 2, src, Dt), BF),
        pltpu.VMEM((T - 1, rows, D), BF),
        pltpu.VMEM((T - 1, rows, D), BF),
        pltpu.VMEM((rows, D), F32),
    ]
    scratch += [pltpu.VMEM((h[0], h[1], 2, EB, LANES), F32) for h in halves]
    scratch += [pltpu.VMEM(h, BF) for h in halves]
    scratch += [pltpu.VMEM(h, BF) for h in halves]
    for shape in ((T,), (T,), (2, WIN), (pairs, WIN), (pairs, T), (T,), (nbits, pairs)):
        scratch += [pltpu.SemaphoreType.DMA(shape)] * 2
    vmem = pl.BlockSpec(memory_space=pltpu.VMEM)
    out, qg, kg, vg, wgt = pl.pallas_call(
        functools.partial(kernel, N, T, nbits),
        out_shape=(
            jax.ShapeDtypeStruct((rows, D), BF),
            jax.ShapeDtypeStruct((rows, D), BF),
            jax.ShapeDtypeStruct((src, Dt), BF),
            jax.ShapeDtypeStruct((src, Dt), BF),
            jax.ShapeDtypeStruct((EB, Dt), BF),
        ),
        in_specs=[pl.BlockSpec(memory_space=pltpu.HBM)] * 5,
        out_specs=(vmem,) * 5,
        scratch_shapes=scratch,
        compiler_params=pltpu.CompilerParams(
            collective_id=0, has_side_effects=True, vmem_limit_bytes=64 * 1024 * 1024 - 64 * 1024
        ),
    )(queries, keys, values, out_weight, out_grad)
    results = (out, qg, kg, vg, wgt)
    out, qg, kg, vg, wgt = pl.pallas_call(
        store_kernel,
        out_shape=tuple(jax.ShapeDtypeStruct(r.shape, r.dtype) for r in results),
        in_specs=[pl.BlockSpec(memory_space=pl.ANY)] * 5,
        out_specs=(pl.BlockSpec(memory_space=pltpu.HBM),) * 5,
        scratch_shapes=[pltpu.SemaphoreType.DMA((5,))],
    )(*results)
    return out, qg, kg, vg, wgt.T


def solution(mesh):
    return jax.shard_map(
        local,
        mesh=mesh,
        in_specs=(
            P(("blk", "tgt"), None),
            P("blk", None),
            P("blk", None),
            P("tgt", None),
            P(("blk", "tgt"), None),
        ),
        out_specs=(
            P(("blk", "tgt"), None),
            P(("blk", "tgt"), None),
            P("blk", "tgt"),
            P("blk", "tgt"),
            P("tgt", "blk"),
        ),
        check_vma=False,
    )
```

```python
import functools

import jax
import jax.numpy as jnp
from jax import lax
from jax.experimental import pallas as pl
from jax.experimental.pallas import tpu as pltpu
from jax.sharding import PartitionSpec as P

HD = 64
WIN = 5
LANES = 128
BF = jnp.bfloat16
F32 = jnp.float32
MESH = pl.DeviceIdType.MESH


def dot(a, b, ca, cb):
    return lax.dot_general(a, b, (((ca,), (cb,)), ((), ())), preferred_element_type=F32)


def kernel(
    N,
    T,
    nbits,
    q_ref,
    k_ref,
    v_ref,
    w_ref,
    og_ref,
    out_ref,
    qg_ref,
    kg_ref,
    vg_ref,
    wgt_ref,
    qall,
    ogall,
    ogt,
    kall,
    vall,
    wv,
    in_s,
    ag,
    att,
    qgs,
    kvown,
    kvs,
    kvr,
    outs,
    outr,
    outown,
    *rest,
):
    acc = rest[:nbits]
    ws = rest[nbits : 2 * nbits]
    wr = rest[2 * nbits : 3 * nbits]
    q_ss, q_rs, og_ss, og_rs, kv_ss, kv_rs, kvg_ss, kvg_rs, qg_ss, qg_rs, o_ss, o_rs, w_ss, w_rs = rest[
        3 * nbits :
    ]
    b = lax.axis_index("blk")
    t = lax.axis_index("tgt")
    rows, D = q_ref.shape
    Dt = w_ref.shape[0]
    R = rows * T
    src = k_ref.shape[0]
    pairs = Dt // LANES
    EB = D // N
    scale = HD ** (-0.5)

    def blk_at(step):
        return lax.rem(b + step + N, N)

    def tgt_at(step):
        return lax.rem(t + step + T, T)

    def bit(k):
        return lax.rem(b // (1 << k), 2)

    def mirror(k):
        return b + (1 - 2 * bit(k)) * (1 << k)

    def cols(tt):
        return pl.ds(pl.multiple_of(tt * Dt, LANES), Dt)

    def tile(tt):
        return pl.ds(pl.multiple_of(tt * rows, LANES), rows)

    def lanes(p, base=0):
        return pl.ds(pl.multiple_of(base + p * LANES, LANES), LANES)

    def remote(src_, dst_, ss, rs, dev):
        return pltpu.make_async_remote_copy(
            src_ref=src_, dst_ref=dst_, send_sem=ss, recv_sem=rs, device_id=dev, device_id_type=MESH
        )

    def q_copy(p, d):
        other = tgt_at(d)
        return remote(
            q_ref.at[:, lanes(p, other * Dt)],
            qall.at[tile(t), lanes(p)],
            q_ss.at[p, d],
            q_rs.at[p, d],
            (b, other),
        )

    def og_copy(d):
        return remote(og_ref, ogall.at[tile(t), :], og_ss.at[d], og_rs.at[d], (b, tgt_at(d)))

    def kv_copy(p, i, w):
        ref, dst = ((k_ref, kall), (v_ref, vall))[i]
        return remote(
            ref.at[:, lanes(p, t * Dt)],
            dst.at[pl.ds(w * src, src), lanes(p)],
            kv_ss.at[p, i, w],
            kv_rs.at[p, i, w],
            (blk_at(w), t),
        )

    def kvg_copy(p, w):
        return remote(
            kvs.at[w - 1, :, :, lanes(p)],
            kvr.at[w - 1, :, :, lanes(p)],
            kvg_ss.at[p, w],
            kvg_rs.at[p, w],
            (blk_at(-w), t),
        )

    def qg_copy(p, d):
        other = tgt_at(d)
        return remote(
            qgs.at[tile(other), lanes(p)],
            qg_ref.at[:, lanes(p, t * Dt)],
            qg_ss.at[p, d],
            qg_rs.at[p, d],
            (b, other),
        )

    def o_copy(d):
        return remote(outs.at[d - 1], outr.at[d - 1], o_ss.at[d], o_rs.at[d], (b, tgt_at(d)))

    def w_copy(k, p):
        return remote(ws[k].at[p], wr[k].at[p], w_ss.at[k, p], w_rs.at[k, p], (mirror(k), t))

    own = [
        pltpu.make_async_copy(s, d, in_s.at[i])
        for i, (s, d) in enumerate(
            (
                (og_ref, ogall.at[tile(t), :]),
                (w_ref, wv),
                (q_ref.at[:, cols(t)], qall.at[tile(t), :]),
                (k_ref.at[:, cols(t)], kall.at[pl.ds(0, src), :]),
                (v_ref.at[:, cols(t)], vall.at[pl.ds(0, src), :]),
            )
        )
    ]
    for copy in own:
        copy.start()

    barrier = pltpu.get_barrier_semaphore()
    peers = [(b, tgt_at(d)) for d in range(1, T)]
    for w in range(1, WIN):
        peers += [(blk_at(w), t), (blk_at(-w), t)]
    for k in range(3, nbits):
        peers.append((mirror(k), t))
    for peer in peers:
        pl.semaphore_signal(barrier, inc=1, device_id=peer, device_id_type=MESH)
    pl.semaphore_wait(barrier, len(peers))

    for d in range(1, T):
        og_copy(d).start()
    for p in range(pairs):
        for w in range(WIN - 1, 0, -1):
            kv_copy(p, 0, w).start()
            kv_copy(p, 1, w).start()
        for d in range(1, T):
            q_copy(p, d).start()

    def project(tt):
        part = ogall[tile(tt), :]
        ag[tile(tt), :] = dot(part, wv[...], 1, 1).astype(BF)
        ogt[:, tile(tt)] = part.astype(F32).T.astype(BF)

    for copy in own:
        copy.wait()
    project(t)
    for d in range(1, T):
        og_copy(d).wait_recv()
        project(tgt_at(-d))
    half = lax.broadcasted_iota(jnp.int32, (1, LANES), 1) // HD

    def fold(k, p):
        w_copy(k, p).wait_recv()
        value = acc[k][p, :, bit(k)] + wr[k][p].astype(F32)
        if k + 1 < nbits:
            acc[k + 1][p] = value.reshape(N >> (k + 2), 2, EB, LANES)
            ws[k + 1][p] = acc[k + 1][p, :, 1 - bit(k + 1)].astype(BF)
            w_copy(k + 1, p).start()
        else:
            wgt_ref[:, lanes(p)] = value[0].astype(BF)

    def pair(p, carry):
        c = lanes(p)
        for d in range(1, T):
            q_copy(p, d).wait_recv()
        for w in range(WIN - 1, 0, -1):
            kv_copy(p, 0, w).wait_recv()
            kv_copy(p, 1, w).wait_recv()
        kp, vp, qp, gp = kall[:, c], vall[:, c], qall[:, c], ag[:, c]
        att_t = jnp.zeros((LANES, R), F32)
        qg_t = jnp.zeros((LANES, R), F32)
        kg = jnp.zeros((WIN * src, LANES), F32)
        vg = jnp.zeros((WIN * src, LANES), F32)
        for i in range(2):
            mask = (half == i).astype(F32).astype(BF)
            km, vm, qm, gm = kp * mask, vp * mask, qp * mask, gp * mask
            scores = dot(km, qp, 1, 1) * scale
            expo = jnp.exp(scores - jnp.max(scores, axis=0, keepdims=True))
            probs = expo * (1.0 / jnp.sum(expo, axis=0, keepdims=True))
            low = probs.astype(BF)
            prob_grad = dot(vm, gp, 1, 1)
            center = jnp.sum(probs * prob_grad, axis=0, keepdims=True)
            score_grad = (scale * probs * (prob_grad - center)).astype(BF)
            att_t += dot(vm, low, 0, 0)
            qg_t += dot(km, score_grad, 0, 0)
            kg += dot(score_grad, qm, 1, 0)
            vg += dot(low, gm, 1, 0)
        att_low = att_t.astype(BF)
        grad = dot(ogt[...], att_low, 1, 1)
        acc[0][p] = grad.reshape(N // 2, 2, EB, LANES)
        ws[0][p] = acc[0][p, :, 1 - bit(0)].astype(BF)
        w_copy(0, p).start()
        kvown[0, :, c] = kg[:src]
        kvown[1, :, c] = vg[:src]
        for w in range(1, WIN):
            kvs[w - 1, 0, :, c] = kg[w * src : (w + 1) * src].astype(BF)
            kvs[w - 1, 1, :, c] = vg[w * src : (w + 1) * src].astype(BF)
            kvg_copy(p, w).start()
        qgs[:, c] = qg_t.T.astype(BF)
        for d in range(1, T):
            qg_copy(p, d).start()
        att[:, c] = att_t.T.astype(BF)

        @pl.when(p >= 1)
        def _():
            fold(0, p - 1)

        @pl.when(p >= 2)
        def _():
            fold(1, p - 2)

        return carry

    lax.fori_loop(0, pairs, pair, 0)

    fold(0, pairs - 1)
    for d in range(1, T):
        outs[d - 1] = dot(att[tile(tgt_at(d)), :], wv[...], 1, 0).astype(BF)
        o_copy(d).start()
    for p in range(max(pairs - 2, 0), pairs):
        fold(1, p)
    outown[...] = dot(att[tile(t), :], wv[...], 1, 0)
    qg_ref[:, cols(t)] = qgs[tile(t), :]
    for k in range(2, nbits):
        for p in range(pairs):
            fold(k, p)
        if k == 2:
            for p in range(pairs):
                for w in range(1, WIN):
                    kvg_copy(p, w).wait_recv()
            for i, ref in enumerate((kg_ref, vg_ref)):
                total = kvown[i]
                for w in range(1, WIN):
                    total += kvr[w - 1, i].astype(F32)
                ref[...] = total.astype(BF)
    total = outown[...]
    for d in range(1, T):
        o_copy(d).wait_recv()
        total += outr[d - 1].astype(F32)
    out_ref[...] = total.astype(BF)
    for p in range(pairs):
        for d in range(1, T):
            qg_copy(p, d).wait_recv()

    for d in range(1, T):
        og_copy(d).wait_send()
        o_copy(d).wait_send()
    for p in range(pairs):
        for w in range(1, WIN):
            kv_copy(p, 0, w).wait_send()
            kv_copy(p, 1, w).wait_send()
            kvg_copy(p, w).wait_send()
        for d in range(1, T):
            q_copy(p, d).wait_send()
            qg_copy(p, d).wait_send()
        for k in range(nbits):
            w_copy(k, p).wait_send()


def store_kernel(*refs):
    for i in range(5):
        refs[5 + i][...] = refs[i][...]


def local(queries, keys, values, out_weight, out_grad):
    N = lax.axis_size("blk")
    T = lax.axis_size("tgt")
    nbits = N.bit_length() - 1
    rows, D = queries.shape
    src = keys.shape[0]
    Dt = out_weight.shape[0]
    R = rows * T
    pairs = Dt // LANES
    EB = D // N
    halves = [(pairs, N >> (k + 1), EB, LANES) for k in range(nbits)]
    scratch = [
        pltpu.VMEM((R, Dt), BF),
        pltpu.VMEM((R, D), BF),
        pltpu.VMEM((D, R), BF),
        pltpu.VMEM((WIN * src, Dt), BF),
        pltpu.VMEM((WIN * src, Dt), BF),
        pltpu.VMEM((Dt, D), BF),
        pltpu.SemaphoreType.DMA((5,)),
        pltpu.VMEM((R, Dt), BF),
        pltpu.VMEM((R, Dt), BF),
        pltpu.VMEM((R, Dt), BF),
        pltpu.VMEM((2, src, Dt), F32),
        pltpu.VMEM((WIN - 1, 2, src, Dt), BF),
        pltpu.VMEM((WIN - 1, 2, src, Dt), BF),
        pltpu.VMEM((T - 1, rows, D), BF),
        pltpu.VMEM((T - 1, rows, D), BF),
        pltpu.VMEM((rows, D), F32),
    ]
    scratch += [pltpu.VMEM((h[0], h[1], 2, EB, LANES), F32) for h in halves]
    scratch += [pltpu.VMEM(h, BF) for h in halves]
    scratch += [pltpu.VMEM(h, BF) for h in halves]
    for shape in ((pairs, T), (T,), (pairs, 2, WIN), (pairs, WIN), (pairs, T), (T,), (nbits, pairs)):
        scratch += [pltpu.SemaphoreType.DMA(shape)] * 2
    vmem = pl.BlockSpec(memory_space=pltpu.VMEM)
    out, qg, kg, vg, wgt = pl.pallas_call(
        functools.partial(kernel, N, T, nbits),
        out_shape=(
            jax.ShapeDtypeStruct((rows, D), BF),
            jax.ShapeDtypeStruct((rows, D), BF),
            jax.ShapeDtypeStruct((src, Dt), BF),
            jax.ShapeDtypeStruct((src, Dt), BF),
            jax.ShapeDtypeStruct((EB, Dt), BF),
        ),
        in_specs=[pl.BlockSpec(memory_space=pltpu.HBM)] * 5,
        out_specs=(vmem,) * 5,
        scratch_shapes=scratch,
        compiler_params=pltpu.CompilerParams(
            collective_id=0, has_side_effects=True, vmem_limit_bytes=64 * 1024 * 1024 - 64 * 1024
        ),
    )(queries, keys, values, out_weight, out_grad)
    results = (out, qg, kg, vg, wgt)
    out, qg, kg, vg, wgt = pl.pallas_call(
        store_kernel,
        out_shape=tuple(jax.ShapeDtypeStruct(r.shape, r.dtype) for r in results),
        in_specs=[vmem] * 5,
        out_specs=(vmem,) * 5,
    )(*results)
    return out, qg, kg, vg, wgt.T


def solution(mesh):
    return jax.shard_map(
        local,
        mesh=mesh,
        in_specs=(
            P(("blk", "tgt"), None),
            P("blk", None),
            P("blk", None),
            P("tgt", None),
            P(("blk", "tgt"), None),
        ),
        out_specs=(
            P(("blk", "tgt"), None),
            P(("blk", "tgt"), None),
            P("blk", "tgt"),
            P("blk", "tgt"),
            P("tgt", "blk"),
        ),
        check_vma=False,
    )
```
